32 devices in a mesh: lens: 2 (over y), gx: 16 (over z, x, core).
Axes of the slice: x: 2, y: 2, z: 4, core: 2. Of those that a mesh axis runs over, the one named last changes fastest.
Arguments:
- electric_init: float32 [3, 512, 24, 512], P(None, ('lens', 'gx')), parts along dimension 1, may hold values from -6 to 6
- magnetic_init: float32 [3, 512, 24, 512], P(None, ('lens', 'gx')), parts along dimension 1, may hold values from -6 to 6
- material: int32 [512, 24, 512], P(('lens', 'gx')), parts along dimension 0, may hold values from 0 to 3
- permittivity: float32 [8], P('lens'), parts along dimension 0, may hold values from 1 to 12
- monitor: int32 [2], P('lens'), parts along dimension 0, may hold values from 2 to 21
Outputs:
- electric: float32 [3, 512, 24, 512], P(None, ('lens', 'gx')), parts along dimension 1
- far_field: float32 [1024, 4, 2, 1024], P('gx', 'lens'), parts along dimension 1
The draws below stay inside these ranges and needn't reach their ends.
There are 2 independent parts, one for each index of `lens`. The reference program is written for one: setup_inputs(seed, part) draws one part's arguments, and reference() takes and returns one part's arrays. A program takes and returns all parts, laid end to end along the dimension named above; each array names one. Nothing has to cross between parts.
Inputs may be any that keep to these rules, and one draw needn't show every extreme that they name: Each design's monitor plane lies inside the slab.
All inputs are finite; a program needn't handle non-finite values.
Results may differ from the reference program's by a relative error of at most 0.0001.
Values sent between devices are 32-bit elements; how exact they have to be, the bound alone decides.
A program may use at most 128 MiB of HBM per device.

```python
import math
import jax
import jax.numpy as jnp
from jax import lax

NY = 512
NZ = 24
STEPS = 4
NMAT = 4
KX = 1024
KY = 1024
NX = 256


def plant(values, key, low, high):
    shape = values.shape
    place = [jax.random.randint(jax.random.fold_in(key, axis), (), 0, shape[axis]) for axis in range(len(shape))]
    values = values.at[tuple(place)].set(low)
    longest = shape.index(max(shape))
    place[longest] = (place[longest] + 1) % shape[longest]
    return values.at[tuple(place)].set(high)


def levels(rng, shape, pieces, smallest, top_value):
    loudness = 1.0
    for dim, shards_of in pieces:
        steps = jax.random.uniform(jax.random.fold_in(jax.random.fold_in(rng, 6), dim), (shards_of,), jnp.float32, smallest / len(pieces), top_value / len(pieces))
        loudness = loudness * jnp.repeat(jnp.exp(steps), shape[dim] // shards_of).reshape((-1,) + (1,) * (len(shape) - 1 - dim))
    return loudness


def centred(stream_key, dims, spread, bound, split=(), held_as=jnp.bfloat16):
    drawn = jax.random.normal(stream_key, dims, jnp.float32) * spread
    if len(split) > 0:
        drawn = levels(stream_key, dims, split, -0.22, 0.18) * drawn
    return jnp.clip(drawn, min=-bound, max=bound).astype(held_as)


def setup_inputs(seed: int = 0, part: int = 0) -> dict:
    keys = jax.random.split(jax.random.key(seed), 6)
    part_splits = jax.random.split(jax.random.fold_in(keys[5], part), 6)
    return {
        "electric_init": centred(part_splits[0], (3, NX, NZ, NY), 1.0, 6.0, ((1, 16),), jnp.float32),
        "magnetic_init": centred(part_splits[1], (3, NX, NZ, NY), 1.0, 6.0, ((1, 16),), jnp.float32),
        "material": plant(jax.random.randint(part_splits[2], (NX, NZ, NY), 0, NMAT), jax.random.fold_in(part_splits[2], 1), 0, NMAT - 1).astype(jnp.int32),
        "permittivity": jnp.clip(jnp.exp(jax.random.uniform(part_splits[3], (NMAT,), jnp.float32, math.log(1.0), math.log(12.0))), 1.0, 12.0),
        "monitor": jax.random.randint(part_splits[4], (1,), 2, NZ - 2).astype(jnp.int32),
    }


courant = 0.55


def diff_up(values, axis):
    widths = [(0, 0)] * values.ndim
    widths[axis] = (0, 1)
    padded = jnp.pad(values, widths)
    return lax.slice_in_dim(padded, 1, padded.shape[axis], axis=axis) - values


def diff_down(values, axis):
    widths = [(0, 0)] * values.ndim
    widths[axis] = (1, 0)
    padded = jnp.pad(values, widths)
    return values - lax.slice_in_dim(padded, 0, values.shape[axis], axis=axis)


def magnetic_step(elec, magn):
    new_x = magn[0] - courant * (diff_up(elec[2], 2) - diff_up(elec[1], 1))
    new_y = magn[1] - courant * (diff_up(elec[0], 1) - diff_up(elec[2], 0))
    new_z = magn[2] - courant * (diff_up(elec[1], 0) - diff_up(elec[0], 2))
    return jnp.stack([new_x, new_y, new_z])


def electric_step(elec, magn, inv_eps):
    new_x = elec[0] + courant * inv_eps * (diff_down(magn[2], 2) - diff_down(magn[1], 1))
    new_y = elec[1] + courant * inv_eps * (diff_down(magn[0], 1) - diff_down(magn[2], 0))
    new_z = elec[2] + courant * inv_eps * (diff_down(magn[1], 0) - diff_down(magn[0], 2))
    return jnp.stack([new_x, new_y, new_z])


def direction_table(count, positions):
    index = jnp.arange(count, dtype=jnp.int32)
    slope = 2 * index + 1 - count
    turns = jnp.remainder(slope[:, None] * positions[None, :], 2 * count)
    angle = turns.astype(jnp.float32) * (math.pi / count)
    return jnp.cos(angle), jnp.sin(angle)


def reference(electric_init, magnetic_init, material, permittivity, monitor):
    inv_table = 1.0 / permittivity
    inv_eps = jnp.take(inv_table, material)
    elec, magn = electric_init, magnetic_init
    for repeat in range(STEPS):
        magn = magnetic_step(elec, magn)
        elec = electric_step(elec, magn, inv_eps)
    plane = lax.dynamic_slice_in_dim(elec[0:2], monitor[0], 1, axis=2)[:, :, 0, :]
    full_x = plane.shape[1]
    full_y = plane.shape[2]
    scale = 1.0 / (float(full_x) * float(full_y)) ** 0.5
    cos_y, sin_y = direction_table(KY, jnp.arange(full_y, dtype=jnp.int32))
    cos_x, sin_x = direction_table(KX, jnp.arange(full_x, dtype=jnp.int32))
    high = lax.Precision.HIGHEST
    near_re = jnp.einsum('cxy,ky->cxk', plane, cos_y, precision=high) * scale
    near_im = -jnp.einsum('cxy,ky->cxk', plane, sin_y, precision=high) * scale
    far_re = jnp.einsum('kx,cxj->kcj', cos_x, near_re, precision=high) + jnp.einsum('kx,cxj->kcj', sin_x, near_im, precision=high)
    far_im = jnp.einsum('kx,cxj->kcj', cos_x, near_im, precision=high) - jnp.einsum('kx,cxj->kcj', sin_x, near_re, precision=high)
    return elec, jnp.stack([far_re, far_im], axis=2)
```

```python
import functools
import math

import jax
import jax.numpy as jnp
import ml_dtypes
import numpy as np
from jax import lax
from jax.experimental import pallas as pl
from jax.experimental.pallas import tpu as pltpu
from jax.sharding import PartitionSpec as P

STEPS = 4
KX = 1024
KY = 1024
COURANT = 0.55
MESH = pl.DeviceIdType.MESH


def fdtd_kernel(
    n, e_in, h_in, mat_in, perm, mon, e_out, plane_out,
    E, H, CE, mat, low_e, low_h, up_e, G,
    load_sem, up_send, up_recv, dn_send, dn_recv, h0_send, h0_recv,
    ring_send, ring_recv, sib_send, sib_recv, out_sem,
):
    bx, nz, ny = E.shape[1:]
    me = lax.axis_index("gx")
    has_low, has_up = me > 0, me < n - 1
    chips = n // 2
    reach = chips // 2
    core, chip = me % 2, me // 2
    column, height = chip % 2, chip // 2
    place = height + column * (chips - 1 - 2 * height)

    def device_at(p, which):
        p = (p + 2 * chips) % chips
        back = p // reach
        at = (1 - back) * (2 * p) + back * (2 * (chips - 1 - p) + 1)
        return 2 * at + which

    ahead, behind = device_at(place + 1, core), device_at(place - 1, core)
    sibling = 2 * chip + (1 - core)

    barrier = pltpu.get_barrier_semaphore()

    def greet(other):
        pl.semaphore_signal(barrier, inc=1, device_id={"gx": other}, device_id_type=MESH)

    loads = [
        pltpu.make_async_copy(e_in, E, load_sem.at[0]),
        pltpu.make_async_copy(h_in, H, load_sem.at[1]),
        pltpu.make_async_copy(mat_in, mat, load_sem.at[2]),
    ]
    for other in (ahead, behind, sibling, (me + 1) % n, (me + n - 1) % n):
        greet(other)

    for load in (loads[2], loads[0], loads[1]):
        load.start()

    @pl.when(me == 0)
    def _():
        low_e[...] = jnp.zeros_like(low_e)
        low_h[...] = jnp.zeros_like(low_h)

    @pl.when(me == n - 1)
    def _():
        up_e[...] = jnp.zeros_like(up_e)

    pl.semaphore_wait(barrier, 5)

    def remote(src, dst, send, recv, other):
        return pltpu.make_async_remote_copy(
            src_ref=src, dst_ref=dst, send_sem=send, recv_sem=recv,
            device_id={"gx": other}, device_id_type=MESH,
        )

    def to_upper(r):
        src = e_in if r == 0 else E
        return remote(src.at[:, bx - 1], low_e.at[r], up_send.at[r], up_recv.at[r], me + 1)

    def to_lower(r):
        src = e_in if r == 0 else E
        return remote(src.at[1:3, 0], up_e.at[r], dn_send.at[r], dn_recv.at[r], me - 1)

    def first_h():
        return remote(h_in.at[1:3, bx - 1], low_h, h0_send, h0_recv, me + 1)

    @pl.when(has_up)
    def _():
        to_upper(0).start()
        first_h().start()

    @pl.when(has_low)
    def _():
        to_lower(0).start()

    lane = lax.broadcasted_iota(jnp.int32, (nz, ny), 1)
    row = lax.broadcasted_iota(jnp.int32, (nz, ny), 0)

    def next_y(v):
        return jnp.where(lane == ny - 1, 0.0, pltpu.roll(v, ny - 1, 1))

    def prev_y(v):
        return jnp.where(lane == 0, 0.0, pltpu.roll(v, 1, 1))

    def next_z(v):
        return jnp.where(row == nz - 1, 0.0, pltpu.roll(v, nz - 1, 0))

    def prev_z(v):
        return jnp.where(row == 0, 0.0, pltpu.roll(v, 1, 0))

    def step_h(x, ey_next, ez_next):
        ex, ey, ez = E[0, x], E[1, x], E[2, x]
        H[0, x] = H[0, x] - COURANT * ((next_y(ez) - ez) - (next_z(ey) - ey))
        H[1, x] = H[1, x] - COURANT * ((next_z(ex) - ex) - (ez_next - ez))
        H[2, x] = H[2, x] - COURANT * ((ey_next - ey) - (next_y(ex) - ex))

    def step_e(x, hy_prev, hz_prev):
        hx, hy, hz = H[0, x], H[1, x], H[2, x]
        ce = CE[x]
        E[0, x] = E[0, x] + ce * ((hz - prev_y(hz)) - (hy - prev_z(hy)))
        E[1, x] = E[1, x] + ce * ((hx - prev_z(hx)) - (hz - hz_prev))
        E[2, x] = E[2, x] + ce * ((hy - hy_prev) - (hx - prev_y(hx)))

    loads[2].wait()
    inverse = [COURANT * (1.0 / jnp.full((1, ny), perm[i], jnp.float32)) for i in range(perm.shape[0])]

    def coefficients(x, carry):
        index = mat[x]
        value = jnp.broadcast_to(inverse[-1], (nz, ny))
        for i in range(len(inverse) - 2, -1, -1):
            value = jnp.where(index == i, inverse[i], value)
        CE[x] = value
        return carry

    lax.fori_loop(0, bx, coefficients, 0)
    loads[0].wait()
    loads[1].wait()
    low_c = jnp.where(me > 0, COURANT, 0.0)

    def inner(x, carry):
        step_h(x, E[1, x + 1], E[2, x + 1])
        step_e(x, H[1, x - 1], H[2, x - 1])
        return carry

    for r in range(STEPS):
        step_h(0, E[1, 1], E[2, 1])
        lax.fori_loop(1, bx - 1, inner, 0)

        @pl.when(has_low)
        def _():
            to_lower(r).wait_send()
            to_upper(r).wait_recv()
            if r == 0:
                first_h().wait_recv()

        @pl.when(has_up)
        def _():
            to_upper(r).wait_send()
            if r == 0:
                first_h().wait_send()

        ex, ey, ez = low_e[r, 0], low_e[r, 1], low_e[r, 2]
        hy = low_h[0] - low_c * ((next_z(ex) - ex) - (E[2, 0] - ez))
        hz = low_h[1] - low_c * ((E[1, 0] - ey) - (next_y(ex) - ex))
        low_h[0] = hy
        low_h[1] = hz
        step_e(0, hy, hz)
        if r < STEPS - 1:

            @pl.when(has_low)
            def _():
                to_lower(r + 1).start()

        @pl.when(has_up)
        def _():
            to_lower(r).wait_recv()

        step_h(bx - 1, up_e[r, 0], up_e[r, 1])
        step_e(bx - 1, H[1, bx - 2], H[2, bx - 2])
        if r < STEPS - 1:

            @pl.when(has_up)
            def _():
                to_upper(r + 1).start()

    m = mon[0]
    for c in range(2):
        for x in range(bx):
            G[c, pl.ds(me * bx + x, 1), :] = E[c, x, pl.ds(m, 1), :]
    store = pltpu.make_async_copy(E, e_out, out_sem.at[0])

    def block(owner, c):
        return G.at[c, pl.ds(pl.multiple_of(owner * bx, bx), bx), :]

    def hop(way, s, c):
        owner = device_at(place - (s - 1), core) if way == 0 else device_at(place + (s - 1), core)
        ref = block(owner, c)
        return remote(
            ref, ref, ring_send.at[way, s - 1, c], ring_recv.at[way, s - 1, c], ahead if way == 0 else behind
        )

    def share(way, s, c):
        owner = device_at(place - s, core) if way == 0 else device_at(place + s, core)
        ref = block(owner, c)
        return remote(ref, ref, sib_send.at[way, s, c], sib_recv.at[way, s, c], sibling)

    hops = {(way, s, c) for way in range(2) for s in range(1, reach) for c in range(2)}
    hops |= {(0, reach, 0), (1, reach, 1)}
    for c in range(2):
        for way in range(2):
            if (way, 1, c) in hops:
                hop(way, 1, c).start()
    shares = [(0, 0, 0), (0, 0, 1)]
    for c in range(2):
        share(0, 0, c).start()
    store.start()
    for s in range(1, reach + 1):
        for c in range(2):
            for way in range(2):
                if (way, s, c) in hops:
                    hop(way, s, c).wait_recv()
                    if (way, s + 1, c) in hops:
                        hop(way, s + 1, c).start()
                    share(way, s, c).start()
                    shares.append((way, s, c))
    for item in shares:
        share(*item).wait_recv()
    keep = pltpu.make_async_copy(G, plane_out, out_sem.at[1])
    keep.start()
    for item in sorted(hops):
        hop(*item).wait_send()
    for item in shares:
        share(*item).wait_send()
    keep.wait()
    store.wait()


def split(value):
    high = value.astype(jnp.bfloat16)
    return high, (value - high.astype(jnp.float32)).astype(jnp.bfloat16)


def dot3(a_hi, a_lo, b_hi, b_lo):
    dot = functools.partial(jnp.dot, preferred_element_type=jnp.float32)
    return dot(a_hi, b_hi) + (dot(a_hi, b_lo) + dot(a_lo, b_hi))


def far_kernel(which, plane, x_hi, x_lo, y_hi, y_lo, e_in, e_out, far, l_hi, l_lo, sem):
    step = pl.program_id(0)
    rows = far.shape[0] * 2
    ny = plane.shape[2]
    copy = pltpu.make_async_copy(e_in, e_out, sem)

    @pl.when(step == 0)
    def _():
        copy.start()
        for c in range(2):
            p_hi, p_lo = split(plane[c])
            both = dot3(x_hi[0], x_lo[0], p_hi, p_lo)
            for part in range(2):
                high, low = split(both[part * rows : (part + 1) * rows])
                l_hi[c * rows : (c + 1) * rows, part * ny : (part + 1) * ny] = high
                l_lo[c * rows : (c + 1) * rows, part * ny : (part + 1) * ny] = low

    out = dot3(l_hi[...], l_lo[...], y_hi[...], y_lo[...])
    for c in range(2):
        far[:, c, :, :] = out[c * rows : (c + 1) * rows].reshape(rows // 2, 2, out.shape[1])

    @pl.when(step == pl.num_programs(0) - 1)
    def _():
        copy.wait()


def angles(count, positions):
    slope = 2 * np.arange(count, dtype=np.int64) + 1 - count
    turns = np.mod(slope[:, None] * np.arange(positions, dtype=np.int64)[None, :], 2 * count)
    return turns * (math.pi / count)


def halves(table):
    table = table.astype(np.float32)
    high = table.astype(ml_dtypes.bfloat16)
    return high, (table - high.astype(np.float32)).astype(ml_dtypes.bfloat16)


def tables(groups, full_x, width_y):
    scale = 1.0 / math.sqrt(full_x * width_y)
    angle_x = angles(KX, full_x).reshape(groups, KX // groups, full_x)
    cos_x, sin_x = scale * np.cos(angle_x), scale * np.sin(angle_x)
    shape = (groups, 2 * KX // groups, full_x)
    with_cos = np.stack([cos_x, -sin_x], axis=2).reshape(shape)
    with_sin = np.stack([-sin_x, -cos_x], axis=2).reshape(shape)
    angle_y = angles(KY, width_y)
    return halves(np.concatenate([with_cos, with_sin], axis=1)) + halves(
        np.concatenate([np.cos(angle_y).T, np.sin(angle_y).T], axis=0)
    )


def per_device(groups, electric_init, magnetic_init, material, permittivity, monitor):
    _, bx, nz, ny = electric_init.shape
    full_x = bx * groups
    reach = groups // 4
    f32 = jnp.float32
    anywhere = pl.BlockSpec(memory_space=pl.ANY)
    scalars = pl.BlockSpec(memory_space=pltpu.SMEM)
    dma = pltpu.SemaphoreType.DMA
    elec, plane = pl.pallas_call(
        functools.partial(fdtd_kernel, groups),
        out_shape=(
            jax.ShapeDtypeStruct(electric_init.shape, f32),
            jax.ShapeDtypeStruct((2, full_x, ny), f32),
        ),
        in_specs=[anywhere, anywhere, anywhere, scalars, scalars],
        out_specs=(anywhere, anywhere),
        scratch_shapes=[
            pltpu.VMEM((3, bx, nz, ny), f32),
            pltpu.VMEM((3, bx, nz, ny), f32),
            pltpu.VMEM((bx, nz, ny), f32),
            pltpu.VMEM((bx, nz, ny), jnp.int32),
            pltpu.VMEM((STEPS, 3, nz, ny), f32),
            pltpu.VMEM((2, nz, ny), f32),
            pltpu.VMEM((STEPS, 2, nz, ny), f32),
            pltpu.VMEM((2, full_x, ny), f32),
            dma((3,)),
            dma((STEPS,)),
            dma((STEPS,)),
            dma((STEPS,)),
            dma((STEPS,)),
            dma,
            dma,
            dma((2, reach, 2)),
            dma((2, reach, 2)),
            dma((2, reach + 1, 2)),
            dma((2, reach + 1, 2)),
            dma((2,)),
        ],
        compiler_params=pltpu.CompilerParams(
            collective_id=0, has_side_effects=True, vmem_limit_bytes=40 * 1024 * 1024
        ),
    )(electric_init, magnetic_init, material, permittivity, monitor)

    x_hi, x_lo, y_hi, y_lo = [jnp.asarray(table) for table in tables(groups, full_x, ny)]
    own = KX // groups
    tile = 256
    which = lax.axis_index("gx").astype(jnp.int32).reshape(1)
    electric, far_field = pl.pallas_call(
        far_kernel,
        out_shape=(
            jax.ShapeDtypeStruct(electric_init.shape, f32),
            jax.ShapeDtypeStruct((own, 2, 2, KY), f32),
        ),
        grid_spec=pltpu.PrefetchScalarGridSpec(
            num_scalar_prefetch=1,
            grid=(KY // tile,),
            in_specs=[
                pl.BlockSpec((2, full_x, ny), lambda j, w: (0, 0, 0)),
                pl.BlockSpec((1, 4 * own, full_x), lambda j, w: (w[0], 0, 0)),
                pl.BlockSpec((1, 4 * own, full_x), lambda j, w: (w[0], 0, 0)),
                pl.BlockSpec((2 * ny, tile), lambda j, w: (0, j)),
                pl.BlockSpec((2 * ny, tile), lambda j, w: (0, j)),
                anywhere,
            ],
            out_specs=(
                anywhere,
                pl.BlockSpec((own, 2, 2, tile), lambda j, w: (0, 0, 0, j)),
            ),
            scratch_shapes=[
                pltpu.VMEM((4 * own, 2 * ny), jnp.bfloat16),
                pltpu.VMEM((4 * own, 2 * ny), jnp.bfloat16),
                dma,
            ],
        ),
        compiler_params=pltpu.CompilerParams(vmem_limit_bytes=48 * 1024 * 1024),
    )(which, plane, x_hi, x_lo, y_hi, y_lo, elec)
    return electric, far_field


def solution(mesh):
    return jax.shard_map(
        functools.partial(per_device, mesh.shape["gx"]),
        mesh=mesh,
        in_specs=(
            P(None, ("lens", "gx"), None, None),
            P(None, ("lens", "gx"), None, None),
            P(("lens", "gx"), None, None),
            P("lens"),
            P("lens"),
        ),
        out_specs=(P(None, ("lens", "gx"), None, None), P("gx", "lens", None, None)),
        check_vma=False,
    )
```

```python
import functools
import math

import jax
import jax.numpy as jnp
import ml_dtypes
import numpy as np
from jax import lax
from jax.experimental import pallas as pl
from jax.experimental.pallas import tpu as pltpu
from jax.sharding import PartitionSpec as P

STEPS = 4
KX = 1024
KY = 1024
COURANT = 0.55
MESH = pl.DeviceIdType.MESH


def fdtd_kernel(
    n, e_in, h_in, mat_in, perm_in, mon, e_out, plane_out,
    E, H, CE, mat, low_e, low_h, up_e, own, perm,
    load_sem, up_send, up_recv, dn_send, dn_recv, h0_send, h0_recv,
    z_send, z_recv, x_send, x_recv, sib_send, sib_recv, out_sem,
):
    bx, nz, ny = E.shape[1:]
    me = lax.axis_index("gx")
    has_low, has_up = me > 0, me < n - 1
    levels = n // 4
    core, column, level = me % 2, (me // 2) % 2, me // 4

    def device_at(z, x, c):
        return 4 * ((z + levels) % levels) + 2 * x + c

    mate = device_at(level, 1 - column, core)
    sibling = device_at(level, column, 1 - core)

    barrier = pltpu.get_barrier_semaphore()

    def greet(other):
        pl.semaphore_signal(barrier, inc=1, device_id={"gx": other}, device_id_type=MESH)

    loads = [
        pltpu.make_async_copy(e_in, E, load_sem.at[0]),
        pltpu.make_async_copy(h_in, H, load_sem.at[1]),
        pltpu.make_async_copy(mat_in, mat, load_sem.at[2]),
        pltpu.make_async_copy(perm_in, perm, load_sem.at[3]),
    ]
    lines = [device_at(level + d, column, core) for d in range(1, levels)]
    for other in [mate, sibling, (me + 1) % n, (me + n - 1) % n] + lines:
        greet(other)

    for load in (loads[3], loads[2], loads[0], loads[1]):
        load.start()

    @pl.when(me == 0)
    def _():
        low_e[...] = jnp.zeros_like(low_e)
        low_h[...] = jnp.zeros_like(low_h)

    @pl.when(me == n - 1)
    def _():
        up_e[...] = jnp.zeros_like(up_e)

    pl.semaphore_wait(barrier, levels + 3)

    def remote(src, dst, send, recv, other):
        return pltpu.make_async_remote_copy(
            src_ref=src, dst_ref=dst, send_sem=send, recv_sem=recv,
            device_id={"gx": other}, device_id_type=MESH,
        )

    def to_upper(r):
        src = e_in if r == 0 else E
        return remote(src.at[:, bx - 1], low_e.at[r], up_send.at[r], up_recv.at[r], me + 1)

    def to_lower(r):
        src = e_in if r == 0 else E
        return remote(src.at[1:3, 0], up_e.at[r], dn_send.at[r], dn_recv.at[r], me - 1)

    def first_h():
        return remote(h_in.at[1:3, bx - 1], low_h, h0_send, h0_recv, me + 1)

    @pl.when(has_up)
    def _():
        to_upper(0).start()
        first_h().start()

    @pl.when(has_low)
    def _():
        to_lower(0).start()

    lane = lax.broadcasted_iota(jnp.int32, (nz, ny), 1)
    row = lax.broadcasted_iota(jnp.int32, (nz, ny), 0)

    def next_y(v):
        return jnp.where(lane == ny - 1, 0.0, pltpu.roll(v, ny - 1, 1))

    def prev_y(v):
        return jnp.where(lane == 0, 0.0, pltpu.roll(v, 1, 1))

    def next_z(v):
        return jnp.where(row == nz - 1, 0.0, pltpu.roll(v, nz - 1, 0))

    def prev_z(v):
        return jnp.where(row == 0, 0.0, pltpu.roll(v, 1, 0))

    def new_h(x, ey_next, ez_next):
        ex, ey, ez = E[0, x], E[1, x], E[2, x]
        return (
            H[0, x] - COURANT * ((next_y(ez) - ez) - (next_z(ey) - ey)),
            H[1, x] - COURANT * ((next_z(ex) - ex) - (ez_next - ez)),
            H[2, x] - COURANT * ((ey_next - ey) - (next_y(ex) - ex)),
        )

    def new_e(x, hy_prev, hz_prev):
        hx, hy, hz = H[0, x], H[1, x], H[2, x]
        ce = CE[x]
        return (
            E[0, x] + ce * ((hz - prev_y(hz)) - (hy - prev_z(hy))),
            E[1, x] + ce * ((hx - prev_z(hx)) - (hz - hz_prev)),
            E[2, x] + ce * ((hy - hy_prev) - (hx - prev_y(hx))),
        )

    def put(ref, x, values):
        for c in range(3):
            ref[c, x] = values[c]

    def step_h(x, ey_next, ez_next):
        put(H, x, new_h(x, ey_next, ez_next))

    def step_e(x, hy_prev, hz_prev):
        put(E, x, new_e(x, hy_prev, hz_prev))

    for i in (3, 2):
        loads[i].wait()
    m = mon[0]
    inverse = [COURANT * (1.0 / jnp.full((1, ny), perm[i], jnp.float32)) for i in range(perm.shape[0])]

    def coefficients(x, carry):
        index = mat[x]
        value = jnp.broadcast_to(inverse[-1], (nz, ny))
        for i in range(len(inverse) - 2, -1, -1):
            value = jnp.where(index == i, inverse[i], value)
        CE[x] = value
        return carry

    lax.fori_loop(0, bx, coefficients, 0)
    loads[0].wait()
    loads[1].wait()
    low_c = jnp.where(me > 0, COURANT, 0.0)

    def inner(x, carry):
        ahead = new_h(x + 1, E[1, x + 2], E[2, x + 2])
        here = new_e(x, H[1, x - 1], H[2, x - 1])
        put(H, x + 1, ahead)
        put(E, x, here)
        return carry

    def inner_h(x, carry):
        step_h(x, E[1, x + 1], E[2, x + 1])
        return carry

    def inner_e(x, carry):
        step_e(x, H[1, x - 1], H[2, x - 1])
        return carry

    def block(owner):
        return plane_out.at[:, pl.ds(pl.multiple_of(owner * bx, bx), bx), :]

    def along(d):
        return remote(own, block(me), z_send.at[d], z_recv.at[d], device_at(level + d, column, core))

    def across(d):
        owner = device_at(level - d, column, core)
        return remote(own if d == 0 else block(owner), block(owner), x_send.at[d], x_recv.at[d], mate)

    def share(side, d):
        owner = device_at(level - d, column + side * (1 - 2 * column), core)
        src = own if side == 0 and d == 0 else block(owner)
        return remote(src, block(owner), sib_send.at[side, d], sib_recv.at[side, d], sibling)

    order = sorted(range(1, levels), key=lambda d: (min(d, levels - d), d))
    store = pltpu.make_async_copy(E, e_out, out_sem.at[0])
    keep = pltpu.make_async_copy(own, block(me), out_sem.at[1])

    for r in range(STEPS):
        last = r == STEPS - 1
        if last:
            lax.fori_loop(0, bx - 1, inner_h, 0)
        else:
            step_h(0, E[1, 1], E[2, 1])
            step_h(1, E[1, 2], E[2, 2])
            lax.fori_loop(1, bx - 2, inner, 0)
            step_e(bx - 2, H[1, bx - 3], H[2, bx - 3])

        @pl.when(has_low)
        def _():
            to_lower(r).wait_send()
            to_upper(r).wait_recv()
            if r == 0:
                first_h().wait_recv()

        @pl.when(has_up)
        def _():
            to_upper(r).wait_send()
            if r == 0:
                first_h().wait_send()

        ex, ey, ez = low_e[r, 0], low_e[r, 1], low_e[r, 2]
        hy = low_h[0] - low_c * ((next_z(ex) - ex) - (E[2, 0] - ez))
        hz = low_h[1] - low_c * ((E[1, 0] - ey) - (next_y(ex) - ex))
        low_h[0] = hy
        low_h[1] = hz
        if not last:
            step_e(0, hy, hz)

            @pl.when(has_low)
            def _():
                to_lower(r + 1).start()

        @pl.when(has_up)
        def _():
            to_lower(r).wait_recv()

        step_h(bx - 1, up_e[r, 0], up_e[r, 1])
        if not last:
            step_e(bx - 1, H[1, bx - 2], H[2, bx - 2])

            @pl.when(has_up)
            def _():
                to_upper(r + 1).start()

    first = lax.broadcasted_iota(jnp.int32, (1, ny), 1) == 0
    at, under = pl.ds(m, 1), pl.ds(jnp.maximum(m - 1, 0), 1)
    for x in range(bx):
        hx, hy, hz = [H[c, x, at, :] for c in range(3)]
        hz_prev = low_h[1, at, :] if x == 0 else H[2, x - 1, at, :]
        ce = CE[x, at, :]
        side = jnp.where(first, 0.0, pltpu.roll(hz, 1, 1))
        own[0, x : x + 1, :] = E[0, x, at, :] + ce * ((hz - side) - (hy - H[1, x, under, :]))
        own[1, x : x + 1, :] = E[1, x, at, :] + ce * ((hx - H[0, x, under, :]) - (hz - hz_prev))

    across(0).start()
    for d in order[::-1]:
        along(d).start()
    share(0, 0).start()
    keep.start()
    step_e(0, low_h[0], low_h[1])
    lax.fori_loop(1, bx, inner_e, 0)
    store.start()

    across(0).wait_recv()
    share(1, 0).start()
    for d in order:
        along(d).wait_recv()
        across(d).start()
        share(0, d).start()
    for d in order:
        across(d).wait_recv()
        share(1, d).start()
    for d in [0] + order:
        share(0, d).wait_recv()
        share(1, d).wait_recv()
    for d in [0] + order:
        if d > 0:
            along(d).wait_send()
        across(d).wait_send()
        share(0, d).wait_send()
        share(1, d).wait_send()
    keep.wait()
    store.wait()


def split(value):
    high = value.astype(jnp.bfloat16)
    return high, (value - high.astype(jnp.float32)).astype(jnp.bfloat16)


def dot3(a_hi, a_lo, b_hi, b_lo):
    dot = functools.partial(jnp.dot, preferred_element_type=jnp.float32)
    return dot(a_hi, b_hi) + (dot(a_hi, b_lo) + dot(a_lo, b_hi))


def far_kernel(which, plane, x_hi, x_lo, y_hi, y_lo, e_in, e_out, far, l_hi, l_lo, sem):
    step = pl.program_id(0)
    rows = far.shape[0] * 2
    ny = plane.shape[2]
    copy = pltpu.make_async_copy(e_in, e_out, sem)

    @pl.when(step == 0)
    def _():
        copy.start()
        for c in range(2):
            p_hi, p_lo = split(plane[c])
            both = dot3(x_hi[0], x_lo[0], p_hi, p_lo)
            for part in range(2):
                high, low = split(both[part * rows : (part + 1) * rows])
                l_hi[c * rows : (c + 1) * rows, part * ny : (part + 1) * ny] = high
                l_lo[c * rows : (c + 1) * rows, part * ny : (part + 1) * ny] = low

    out = dot3(l_hi[...], l_lo[...], y_hi[...], y_lo[...])
    for c in range(2):
        far[:, c, :, :] = out[c * rows : (c + 1) * rows].reshape(rows // 2, 2, out.shape[1])

    @pl.when(step == pl.num_programs(0) - 1)
    def _():
        copy.wait()


def angles(count, positions):
    slope = 2 * np.arange(count, dtype=np.int64) + 1 - count
    turns = np.mod(slope[:, None] * np.arange(positions, dtype=np.int64)[None, :], 2 * count)
    return turns * (math.pi / count)


def halves(table):
    table = table.astype(np.float32)
    high = table.astype(ml_dtypes.bfloat16)
    return high, (table - high.astype(np.float32)).astype(ml_dtypes.bfloat16)


def tables(groups, full_x, width_y):
    scale = 1.0 / math.sqrt(full_x * width_y)
    angle_x = angles(KX, full_x).reshape(groups, KX // groups, full_x)
    cos_x, sin_x = scale * np.cos(angle_x), scale * np.sin(angle_x)
    shape = (groups, 2 * KX // groups, full_x)
    with_cos = np.stack([cos_x, -sin_x], axis=2).reshape(shape)
    with_sin = np.stack([-sin_x, -cos_x], axis=2).reshape(shape)
    angle_y = angles(KY, width_y)
    return halves(np.concatenate([with_cos, with_sin], axis=1)) + halves(
        np.concatenate([np.cos(angle_y).T, np.sin(angle_y).T], axis=0)
    )


def per_device(groups, electric_init, magnetic_init, material, permittivity, monitor):
    _, bx, nz, ny = electric_init.shape
    full_x = bx * groups
    levels = groups // 4
    f32 = jnp.float32
    anywhere = pl.BlockSpec(memory_space=pl.ANY)

    def in_hbm(value):
        return pltpu.with_memory_space_constraint(value, pltpu.HBM)

    off_core = pl.BlockSpec(memory_space=pltpu.HBM)
    dma = pltpu.SemaphoreType.DMA
    elec, plane = pl.pallas_call(
        functools.partial(fdtd_kernel, groups),
        out_shape=(
            jax.ShapeDtypeStruct(electric_init.shape, f32),
            jax.ShapeDtypeStruct((2, full_x, ny), f32),
        ),
        in_specs=[off_core] * 4 + [pl.BlockSpec(memory_space=pltpu.SMEM)],
        out_specs=(anywhere, anywhere),
        scratch_shapes=[
            pltpu.VMEM((3, bx, nz, ny), f32),
            pltpu.VMEM((3, bx, nz, ny), f32),
            pltpu.VMEM((bx, nz, ny), f32),
            pltpu.VMEM((bx, nz, ny), jnp.int32),
            pltpu.VMEM((STEPS, 3, nz, ny), f32),
            pltpu.VMEM((2, nz, ny), f32),
            pltpu.VMEM((STEPS, 2, nz, ny), f32),
            pltpu.VMEM((2, bx, ny), f32),
            pltpu.SMEM(permittivity.shape, f32),
            dma((4,)),
            dma((STEPS,)),
            dma((STEPS,)),
            dma((STEPS,)),
            dma((STEPS,)),
            dma,
            dma,
            dma((levels,)),
            dma((levels,)),
            dma((levels,)),
            dma((levels,)),
            dma((2, levels)),
            dma((2, levels)),
            dma((2,)),
        ],
        compiler_params=pltpu.CompilerParams(
            collective_id=0, has_side_effects=True, vmem_limit_bytes=24 * 1024 * 1024
        ),
    )(*map(in_hbm, (electric_init, magnetic_init, material, permittivity)), monitor)

    x_hi, x_lo, y_hi, y_lo = [in_hbm(jnp.asarray(table)) for table in tables(groups, full_x, ny)]
    own = KX // groups
    tile = 256
    which = lax.axis_index("gx").astype(jnp.int32).reshape(1)
    electric, far_field = pl.pallas_call(
        far_kernel,
        out_shape=(
            jax.ShapeDtypeStruct(electric_init.shape, f32),
            jax.ShapeDtypeStruct((own, 2, 2, KY), f32),
        ),
        grid_spec=pltpu.PrefetchScalarGridSpec(
            num_scalar_prefetch=1,
            grid=(KY // tile,),
            in_specs=[
                pl.BlockSpec((2, full_x, ny), lambda j, w: (0, 0, 0)),
                pl.BlockSpec((1, 4 * own, full_x), lambda j, w: (w[0], 0, 0)),
                pl.BlockSpec((1, 4 * own, full_x), lambda j, w: (w[0], 0, 0)),
                pl.BlockSpec((2 * ny, tile), lambda j, w: (0, j)),
                pl.BlockSpec((2 * ny, tile), lambda j, w: (0, j)),
                anywhere,
            ],
            out_specs=(
                anywhere,
                pl.BlockSpec((own, 2, 2, tile), lambda j, w: (0, 0, 0, j)),
            ),
            scratch_shapes=[
                pltpu.VMEM((4 * own, 2 * ny), jnp.bfloat16),
                pltpu.VMEM((4 * own, 2 * ny), jnp.bfloat16),
                dma,
            ],
        ),
        compiler_params=pltpu.CompilerParams(vmem_limit_bytes=28 * 1024 * 1024),
    )(which, plane, x_hi, x_lo, y_hi, y_lo, elec)
    return electric, far_field


def solution(mesh):
    return jax.shard_map(
        functools.partial(per_device, mesh.shape["gx"]),
        mesh=mesh,
        in_specs=(
            P(None, ("lens", "gx"), None, None),
            P(None, ("lens", "gx"), None, None),
            P(("lens", "gx"), None, None),
            P("lens"),
            P("lens"),
        ),
        out_specs=(P(None, ("lens", "gx"), None, None), P("gx", "lens", None, None)),
        check_vma=False,
    )
```

```python
import functools
import math

import jax
import jax.numpy as jnp
import ml_dtypes
import numpy as np
from jax import lax
from jax.experimental import pallas as pl
from jax.experimental.pallas import tpu as pltpu
from jax.sharding import PartitionSpec as P

STEPS = 4
KX = 1024
KY = 1024
COURANT = 0.55
MESH = pl.DeviceIdType.MESH


def fdtd_kernel(
    n, e_in, h_in, mat_in, perm_in, mon, y_hi, y_lo,
    e_out, plane_out, y_hi_out, y_lo_out,
    E, H, CE, mat, low_e, low_h, up_e, own, perm,
    load_sem, up_send, up_recv, dn_send, dn_recv, h0_send, h0_recv,
    z_send, z_recv, x_send, x_recv, sib_send, sib_recv, out_sem,
):
    bx, nz, ny = E.shape[1:]
    me = lax.axis_index("gx")
    has_low, has_up = me > 0, me < n - 1
    levels = n // 4
    core, column, level = me % 2, (me // 2) % 2, me // 4

    def device_at(z, x, c):
        return 4 * ((z + levels) % levels) + 2 * x + c

    mate = device_at(level, 1 - column, core)
    sibling = device_at(level, column, 1 - core)

    barrier = pltpu.get_barrier_semaphore()

    def greet(other):
        pl.semaphore_signal(barrier, inc=1, device_id={"gx": other}, device_id_type=MESH)

    loads = [
        pltpu.make_async_copy(e_in, E, load_sem.at[0]),
        pltpu.make_async_copy(h_in, H, load_sem.at[1]),
        pltpu.make_async_copy(mat_in, mat, load_sem.at[2]),
        pltpu.make_async_copy(perm_in, perm, load_sem.at[3]),
        pltpu.make_async_copy(y_hi, y_hi_out, load_sem.at[4]),
        pltpu.make_async_copy(y_lo, y_lo_out, load_sem.at[5]),
    ]
    lines = [device_at(level + d, column, core) for d in range(1, levels)]
    for other in [mate, sibling, (me + 1) % n, (me + n - 1) % n] + lines:
        greet(other)

    for load in (loads[3], loads[2], loads[0], loads[1]):
        load.start()

    @pl.when(me == 0)
    def _():
        low_e[...] = jnp.zeros_like(low_e)
        low_h[...] = jnp.zeros_like(low_h)

    @pl.when(me == n - 1)
    def _():
        up_e[...] = jnp.zeros_like(up_e)

    pl.semaphore_wait(barrier, levels + 3)

    def remote(src, dst, send, recv, other):
        return pltpu.make_async_remote_copy(
            src_ref=src, dst_ref=dst, send_sem=send, recv_sem=recv,
            device_id={"gx": other}, device_id_type=MESH,
        )

    def to_upper(r):
        src = e_in if r == 0 else E
        return remote(src.at[:, bx - 1], low_e.at[r], up_send.at[r], up_recv.at[r], me + 1)

    def to_lower(r):
        src = e_in if r == 0 else E
        return remote(src.at[1:3, 0], up_e.at[r], dn_send.at[r], dn_recv.at[r], me - 1)

    def first_h():
        return remote(h_in.at[1:3, bx - 1], low_h, h0_send, h0_recv, me + 1)

    @pl.when(has_up)
    def _():
        to_upper(0).start()
        first_h().start()

    @pl.when(has_low)
    def _():
        to_lower(0).start()

    lane = lax.broadcasted_iota(jnp.int32, (nz, ny), 1)
    row = lax.broadcasted_iota(jnp.int32, (nz, ny), 0)

    def next_y(v):
        return jnp.where(lane == ny - 1, 0.0, pltpu.roll(v, ny - 1, 1))

    def prev_y(v):
        return jnp.where(lane == 0, 0.0, pltpu.roll(v, 1, 1))

    def next_z(v):
        return jnp.where(row == nz - 1, 0.0, pltpu.roll(v, nz - 1, 0))

    def prev_z(v):
        return jnp.where(row == 0, 0.0, pltpu.roll(v, 1, 0))

    def new_h(x, ey_next, ez_next):
        ex, ey, ez = E[0, x], E[1, x], E[2, x]
        return (
            H[0, x] - COURANT * ((next_y(ez) - ez) - (next_z(ey) - ey)),
            H[1, x] - COURANT * ((next_z(ex) - ex) - (ez_next - ez)),
            H[2, x] - COURANT * ((ey_next - ey) - (next_y(ex) - ex)),
        )

    def new_e(x, hy_prev, hz_prev):
        hx, hy, hz = H[0, x], H[1, x], H[2, x]
        ce = CE[x]
        return (
            E[0, x] + ce * ((hz - prev_y(hz)) - (hy - prev_z(hy))),
            E[1, x] + ce * ((hx - prev_z(hx)) - (hz - hz_prev)),
            E[2, x] + ce * ((hy - hy_prev) - (hx - prev_y(hx))),
        )

    def put(ref, x, values):
        for c in range(3):
            ref[c, x] = values[c]

    def step_h(x, ey_next, ez_next):
        put(H, x, new_h(x, ey_next, ez_next))

    def step_e(x, hy_prev, hz_prev):
        put(E, x, new_e(x, hy_prev, hz_prev))

    for i in (3, 2):
        loads[i].wait()
    m = mon[0]
    inverse = [COURANT * (1.0 / jnp.full((1, ny), perm[i], jnp.float32)) for i in range(perm.shape[0])]

    def coefficients(x, carry):
        index = mat[x]
        value = jnp.broadcast_to(inverse[-1], (nz, ny))
        for i in range(len(inverse) - 2, -1, -1):
            value = jnp.where(index == i, inverse[i], value)
        CE[x] = value
        return carry

    lax.fori_loop(0, bx, coefficients, 0)
    loads[0].wait()
    loads[1].wait()
    loads[4].start()
    loads[5].start()
    low_c = jnp.where(me > 0, COURANT, 0.0)

    def inner(x, carry):
        ahead = new_h(x + 1, E[1, x + 2], E[2, x + 2])
        here = new_e(x, H[1, x - 1], H[2, x - 1])
        put(H, x + 1, ahead)
        put(E, x, here)
        return carry

    def inner_h(x, carry):
        step_h(x, E[1, x + 1], E[2, x + 1])
        return carry

    def inner_e(x, carry):
        step_e(x, H[1, x - 1], H[2, x - 1])
        return carry

    def block(owner):
        return plane_out.at[:, pl.ds(pl.multiple_of(owner * bx, bx), bx), :]

    def along(d):
        return remote(own, block(me), z_send.at[d], z_recv.at[d], device_at(level + d, column, core))

    def across(d):
        owner = device_at(level - d, column, core)
        return remote(own if d == 0 else block(owner), block(owner), x_send.at[d], x_recv.at[d], mate)

    def share(side, d):
        owner = device_at(level - d, column + side * (1 - 2 * column), core)
        src = own if side == 0 and d == 0 else block(owner)
        return remote(src, block(owner), sib_send.at[side, d], sib_recv.at[side, d], sibling)

    order = sorted(range(1, levels), key=lambda d: (min(d, levels - d), d))
    store = pltpu.make_async_copy(E, e_out, out_sem.at[0])
    keep = pltpu.make_async_copy(own, block(me), out_sem.at[1])

    for r in range(STEPS):
        last = r == STEPS - 1
        if last:
            lax.fori_loop(0, bx - 1, inner_h, 0)
        else:
            step_h(0, E[1, 1], E[2, 1])
            step_h(1, E[1, 2], E[2, 2])
            lax.fori_loop(1, bx - 2, inner, 0)
            step_e(bx - 2, H[1, bx - 3], H[2, bx - 3])

        @pl.when(has_low)
        def _():
            to_lower(r).wait_send()
            to_upper(r).wait_recv()
            if r == 0:
                first_h().wait_recv()

        @pl.when(has_up)
        def _():
            to_upper(r).wait_send()
            if r == 0:
                first_h().wait_send()

        ex, ey, ez = low_e[r, 0], low_e[r, 1], low_e[r, 2]
        hy = low_h[0] - low_c * ((next_z(ex) - ex) - (E[2, 0] - ez))
        hz = low_h[1] - low_c * ((E[1, 0] - ey) - (next_y(ex) - ex))
        low_h[0] = hy
        low_h[1] = hz
        if not last:
            step_e(0, hy, hz)

            @pl.when(has_low)
            def _():
                to_lower(r + 1).start()

        @pl.when(has_up)
        def _():
            to_lower(r).wait_recv()

        step_h(bx - 1, up_e[r, 0], up_e[r, 1])
        if not last:
            step_e(bx - 1, H[1, bx - 2], H[2, bx - 2])

            @pl.when(has_up)
            def _():
                to_upper(r + 1).start()

    first = lax.broadcasted_iota(jnp.int32, (1, ny), 1) == 0
    at, under = pl.ds(m, 1), pl.ds(jnp.maximum(m - 1, 0), 1)
    for x in range(bx):
        hx, hy, hz = [H[c, x, at, :] for c in range(3)]
        hz_prev = low_h[1, at, :] if x == 0 else H[2, x - 1, at, :]
        ce = CE[x, at, :]
        side = jnp.where(first, 0.0, pltpu.roll(hz, 1, 1))
        own[0, x : x + 1, :] = E[0, x, at, :] + ce * ((hz - side) - (hy - H[1, x, under, :]))
        own[1, x : x + 1, :] = E[1, x, at, :] + ce * ((hx - H[0, x, under, :]) - (hz - hz_prev))

    across(0).start()
    for d in order[::-1]:
        along(d).start()
    share(0, 0).start()
    keep.start()
    step_e(0, low_h[0], low_h[1])
    lax.fori_loop(1, bx, inner_e, 0)
    store.start()

    across(0).wait_recv()
    share(1, 0).start()
    for d in order:
        along(d).wait_recv()
        across(d).start()
        share(0, d).start()
    for d in order:
        across(d).wait_recv()
        share(1, d).start()
    for d in [0] + order:
        share(0, d).wait_recv()
        share(1, d).wait_recv()
    for d in [0] + order:
        if d > 0:
            along(d).wait_send()
        across(d).wait_send()
        share(0, d).wait_send()
        share(1, d).wait_send()
    keep.wait()
    store.wait()
    loads[4].wait()
    loads[5].wait()


def split(value):
    high = value.astype(jnp.bfloat16)
    return high, (value - high.astype(jnp.float32)).astype(jnp.bfloat16)


def dot3(a_hi, a_lo, b_hi, b_lo):
    dot = functools.partial(jnp.dot, preferred_element_type=jnp.float32)
    return dot(a_hi, b_hi) + (dot(a_hi, b_lo) + dot(a_lo, b_hi))


def far_kernel(which, plane, x_hi, x_lo, y_hi, y_lo, e_in, e_out, far, l_hi, l_lo, sem):
    step = pl.program_id(0)
    rows = far.shape[0] * 2
    ny = plane.shape[2]
    copy = pltpu.make_async_copy(e_in, e_out, sem)

    @pl.when(step == 0)
    def _():
        copy.start()
        for c in range(2):
            p_hi, p_lo = split(plane[c])
            both = dot3(x_hi[0], x_lo[0], p_hi, p_lo)
            for part in range(2):
                high, low = split(both[part * rows : (part + 1) * rows])
                l_hi[c * rows : (c + 1) * rows, part * ny : (part + 1) * ny] = high
                l_lo[c * rows : (c + 1) * rows, part * ny : (part + 1) * ny] = low

    out = dot3(l_hi[...], l_lo[...], y_hi[...], y_lo[...])
    for c in range(2):
        far[:, c, :, :] = out[c * rows : (c + 1) * rows].reshape(rows // 2, 2, out.shape[1])

    @pl.when(step == pl.num_programs(0) - 1)
    def _():
        copy.wait()


def angles(count, positions):
    slope = 2 * np.arange(count, dtype=np.int64) + 1 - count
    turns = np.mod(slope[:, None] * np.arange(positions, dtype=np.int64)[None, :], 2 * count)
    return turns * (math.pi / count)


def halves(table):
    table = table.astype(np.float32)
    high = table.astype(ml_dtypes.bfloat16)
    return high, (table - high.astype(np.float32)).astype(ml_dtypes.bfloat16)


def tables(groups, full_x, width_y):
    scale = 1.0 / math.sqrt(full_x * width_y)
    angle_x = angles(KX, full_x).reshape(groups, KX // groups, full_x)
    cos_x, sin_x = scale * np.cos(angle_x), scale * np.sin(angle_x)
    shape = (groups, 2 * KX // groups, full_x)
    with_cos = np.stack([cos_x, -sin_x], axis=2).reshape(shape)
    with_sin = np.stack([-sin_x, -cos_x], axis=2).reshape(shape)
    angle_y = angles(KY, width_y)
    return halves(np.concatenate([with_cos, with_sin], axis=1)) + halves(
        np.concatenate([np.cos(angle_y).T, np.sin(angle_y).T], axis=0)
    )


def per_device(groups, electric_init, magnetic_init, material, permittivity, monitor):
    _, bx, nz, ny = electric_init.shape
    full_x = bx * groups
    levels = groups // 4
    f32 = jnp.float32
    anywhere = pl.BlockSpec(memory_space=pl.ANY)

    def in_hbm(value):
        return pltpu.with_memory_space_constraint(value, pltpu.HBM)

    off_core = pl.BlockSpec(memory_space=pltpu.HBM)
    dma = pltpu.SemaphoreType.DMA
    x_hi, x_lo, y_hi, y_lo = [in_hbm(jnp.asarray(table)) for table in tables(groups, full_x, ny)]
    elec, plane, y_hi, y_lo = pl.pallas_call(
        functools.partial(fdtd_kernel, groups),
        out_shape=(
            jax.ShapeDtypeStruct(electric_init.shape, f32),
            jax.ShapeDtypeStruct((2, full_x, ny), f32),
            jax.ShapeDtypeStruct(y_hi.shape, y_hi.dtype),
            jax.ShapeDtypeStruct(y_lo.shape, y_lo.dtype),
        ),
        in_specs=[off_core] * 4 + [pl.BlockSpec(memory_space=pltpu.SMEM)] + [off_core] * 2,
        out_specs=(anywhere,) * 4,
        scratch_shapes=[
            pltpu.VMEM((3, bx, nz, ny), f32),
            pltpu.VMEM((3, bx, nz, ny), f32),
            pltpu.VMEM((bx, nz, ny), f32),
            pltpu.VMEM((bx, nz, ny), jnp.int32),
            pltpu.VMEM((STEPS, 3, nz, ny), f32),
            pltpu.VMEM((2, nz, ny), f32),
            pltpu.VMEM((STEPS, 2, nz, ny), f32),
            pltpu.VMEM((2, bx, ny), f32),
            pltpu.SMEM(permittivity.shape, f32),
            dma((6,)),
            dma((STEPS,)),
            dma((STEPS,)),
            dma((STEPS,)),
            dma((STEPS,)),
            dma,
            dma,
            dma((levels,)),
            dma((levels,)),
            dma((levels,)),
            dma((levels,)),
            dma((2, levels)),
            dma((2, levels)),
            dma((2,)),
        ],
        compiler_params=pltpu.CompilerParams(
            collective_id=0, has_side_effects=True, vmem_limit_bytes=24 * 1024 * 1024
        ),
    )(*map(in_hbm, (electric_init, magnetic_init, material, permittivity)), monitor, y_hi, y_lo)

    own = KX // groups
    tile = 256
    which = lax.axis_index("gx").astype(jnp.int32).reshape(1)
    electric, far_field = pl.pallas_call(
        far_kernel,
        out_shape=(
            jax.ShapeDtypeStruct(electric_init.shape, f32),
            jax.ShapeDtypeStruct((own, 2, 2, KY), f32),
        ),
        grid_spec=pltpu.PrefetchScalarGridSpec(
            num_scalar_prefetch=1,
            grid=(KY // tile,),
            in_specs=[
                pl.BlockSpec((2, full_x, ny), lambda j, w: (0, 0, 0)),
                pl.BlockSpec((1, 4 * own, full_x), lambda j, w: (w[0], 0, 0)),
                pl.BlockSpec((1, 4 * own, full_x), lambda j, w: (w[0], 0, 0)),
                pl.BlockSpec((2 * ny, tile), lambda j, w: (0, j)),
                pl.BlockSpec((2 * ny, tile), lambda j, w: (0, j)),
                anywhere,
            ],
            out_specs=(
                anywhere,
                pl.BlockSpec((own, 2, 2, tile), lambda j, w: (0, 0, 0, j)),
            ),
            scratch_shapes=[
                pltpu.VMEM((4 * own, 2 * ny), jnp.bfloat16),
                pltpu.VMEM((4 * own, 2 * ny), jnp.bfloat16),
                dma,
            ],
        ),
        compiler_params=pltpu.CompilerParams(vmem_limit_bytes=28 * 1024 * 1024),
    )(which, plane, x_hi, x_lo, y_hi, y_lo, elec)
    return electric, far_field


def solution(mesh):
    return jax.shard_map(
        functools.partial(per_device, mesh.shape["gx"]),
        mesh=mesh,
        in_specs=(
            P(None, ("lens", "gx"), None, None),
            P(None, ("lens", "gx"), None, None),
            P(("lens", "gx"), None, None),
            P("lens"),
            P("lens"),
        ),
        out_specs=(P(None, ("lens", "gx"), None, None), P("gx", "lens", None, None)),
        check_vma=False,
    )
```
